512 devices in a mesh: video: 8 (over x, core), frame: 64 (over y, z).
Axes of the slice: x: 4, y: 8, z: 8, core: 2. Of those that a mesh axis runs over, the one named last changes fastest.
Arguments:
- tokens: bfloat16 [8, 128, 256, 1024], P('video', 'frame')
- counts: int32 [8], P('video'), may hold values from 2 to 128, as said below
- frame_index: int32 [8, 128], P('video'), may hold values from 0 to 127, each once within a row
- owner_slot: int32 [8, 128], P('video'), may hold values from 0 to 127, each once within a row
- gain_attn: float32 [1024], replicated
- gain_kv: float32 [1024], replicated, may hold values from 0.1 to 1.9
- slopes: float32 [16], replicated, may hold values from 0.003 to 0.15
- w_qkv: bfloat16 [1024, 3072], P('video', 'frame'), may hold values from -0.1875 to 0.1875
- w_out: bfloat16 [1024, 1024], P(None, 'video'), may hold values from -0.1875 to 0.1875
- w_kv: bfloat16 [1024, 2048], P(None, 'frame'), may hold values from -0.1875 to 0.1875
Outputs:
- res_keys: bfloat16 [8, 128, 256, 1024], P('video', 'frame')
- res_values: bfloat16 [8, 128, 256, 1024], P('video', 'frame')
The draws below stay inside these ranges and needn't reach their ends.
Inputs may be any that keep to these rules, and one draw needn't show every extreme that they name: `frame_index`: each row is an ordering of frames 0 to 128 - 1 over a video's slots; frames at or past counts of that video are padding. `owner_slot`: each row is a permutation of the slots. `counts`: some video has all 128 frames.
All inputs are finite; a program needn't handle non-finite values.
Results may differ from the reference program's by a relative error of at most 0.0076.
Values may be sent and summed in bfloat16 or wider, within the bound.
A program may use at most 64 MiB of HBM per device.

```python
import math
import jax
import jax.numpy as jnp
from jax import lax

D = 1024
HEADS = 16
HD = 64
P_SIZE = 256
FMAX = 128
VIDEOS = 8


def draw_tokens(key, part):
    key = jax.random.fold_in(key, 11)
    first = jax.random.fold_in(key, 0)
    noise = jax.random.normal(first, (VIDEOS, FMAX, P_SIZE, D), jnp.float32)
    values = noise
    return values.astype(jnp.bfloat16)


def draw_counts(key, part):
    key = jax.random.fold_in(key, 12)
    first, second = jax.random.split(key)
    drawn = jax.random.randint(first, (VIDEOS,), 2, FMAX + 1)
    longest = jax.random.randint(second, (), 0, VIDEOS)
    return drawn.at[longest].set(FMAX).astype(jnp.int32)


def draw_gain_attn(key, part):
    key = jax.random.fold_in(key, 13)
    values = jax.random.uniform(key, (D,), jnp.float32, 0.6, 1.6)
    return values


def block_scale(rng, shape, shards, low, top_value):
    def one(position, parts):
        draws = jax.random.uniform(jax.random.fold_in(jax.random.fold_in(rng, 6), position), (parts,), jnp.float32, low / len(shards), top_value / len(shards))
        return jnp.repeat(jnp.exp(draws), shape[position] // parts).reshape((-1,) + (1,) * (len(shape) - position - 1))

    loudness = one(*shards[0])
    for cut in shards[1:]:
        loudness = loudness * one(*cut)
    return loudness


def bell_draw(stream_key, extent, scale, reach, cuts=(), kind=jnp.bfloat16):
    values = scale * jax.random.normal(stream_key, extent, jnp.float32)
    if cuts:
        values = values * block_scale(stream_key, extent, cuts, -0.22, 0.18)
    return jnp.clip(values, -reach, reach).astype(kind)


def setup_inputs(seed: int = 0) -> dict:
    key_of = jax.random.split(jax.random.key(seed), 11)
    tokens = draw_tokens(jax.random.fold_in(key_of[10], 71), 0)
    counts = draw_counts(jax.random.fold_in(key_of[10], 71), 0)
    frame_index = jax.vmap(lambda own: jax.random.permutation(own, FMAX))(jax.random.split(key_of[2], VIDEOS)).reshape((VIDEOS, FMAX)).astype(jnp.int32)
    owner_slot = jax.vmap(lambda own: jax.random.permutation(own, FMAX))(jax.random.split(key_of[3], VIDEOS)).reshape((VIDEOS, FMAX)).astype(jnp.int32)
    gain_attn = draw_gain_attn(jax.random.fold_in(key_of[10], 71), 0)
    gain_kv = jnp.clip(1.0 + 0.18 * jax.random.normal(key_of[5], (D,), jnp.float32), 0.1, 1.9)
    slopes = jnp.clip(jnp.exp(jax.random.uniform(key_of[6], (HEADS,), jnp.float32, math.log(0.003), math.log(0.15))), 0.003, 0.15)
    w_qkv = bell_draw(key_of[7], (D, 3 * D), D ** -0.5, 0.1875, ((0, 8), (1, 64)))
    w_out = bell_draw(key_of[8], (D, D), D ** -0.5, 0.1875, ((1, 8),))
    w_kv = bell_draw(key_of[9], (D, 2 * D), D ** -0.5, 0.1875, ((1, 64),))
    return dict(tokens=tokens, counts=counts, frame_index=frame_index, owner_slot=owner_slot, gain_attn=gain_attn, gain_kv=gain_kv, slopes=slopes, w_qkv=w_qkv, w_out=w_out, w_kv=w_kv)


def layer_norm(rows, gain):
    values = rows.astype(jnp.float32)
    center = lax.optimization_barrier(jnp.mean(values, axis=-1, keepdims=True))
    spread = lax.optimization_barrier(jnp.mean(jnp.square(values - center), axis=-1, keepdims=True))
    return ((values - center) * lax.rsqrt(spread + 1e-05) * gain).astype(jnp.bfloat16)

def reference(tokens, counts, frame_index, owner_slot, gain_attn, gain_kv, slopes, w_qkv, w_out, w_kv):

    def one_video(pack):
        video_tok, count, frame_ids, owners = pack
        normed = layer_norm(video_tok, gain_attn).reshape(-1, D)
        qkv = jnp.dot(normed, w_qkv, preferred_element_type=jnp.float32).astype(jnp.bfloat16)
        qkv = qkv.reshape(FMAX, P_SIZE, 3 * D)
        query = qkv[..., :D].reshape(FMAX, P_SIZE, HEADS, HD).astype(jnp.float32)
        keyed = qkv[..., D:2 * D].reshape(FMAX, P_SIZE, HEADS, HD).astype(jnp.float32)
        valued = qkv[..., 2 * D:].reshape(FMAX, P_SIZE, HEADS, HD).astype(jnp.float32)
        scores = jnp.einsum('sphd,tphd->phst', query, keyed) * HD ** (-0.5)
        times = frame_ids.astype(jnp.float32)
        distance = jnp.abs(times[:, None] - times[None, :])
        scores = scores - slopes[None, :, None, None] * distance[None, None]
        valid = frame_ids < count
        scores = jnp.where(valid[None, None, None, :], scores, -1e+30)
        top = lax.optimization_barrier(jnp.max(scores, axis=-1, keepdims=True))
        expo = jnp.exp(scores - top)
        weights = (expo / lax.optimization_barrier(jnp.sum(expo, axis=-1, keepdims=True))).astype(jnp.bfloat16)
        attended = jnp.einsum('phst,tphd->sphd', weights.astype(jnp.float32), valued)
        attended = attended.astype(jnp.bfloat16).reshape(-1, D)
        updated = (video_tok.reshape(-1, D).astype(jnp.float32) + jnp.dot(attended, w_out, preferred_element_type=jnp.float32)).astype(jnp.bfloat16)
        normed_kv = layer_norm(updated, gain_kv)
        pairs = jnp.dot(normed_kv, w_kv, preferred_element_type=jnp.float32).astype(jnp.bfloat16)
        pairs = pairs.reshape(FMAX, P_SIZE, 2 * D)
        pairs = jnp.where(valid[:, None, None], pairs, jnp.zeros_like(pairs))
        placed = jnp.zeros_like(pairs).at[owners].set(pairs)
        return (placed[..., :D], placed[..., D:])
    res_keys, res_values = lax.map(one_video, (tokens, counts, frame_index, owner_slot))
    return (res_keys, res_values)
```

```python
import jax
import jax.numpy as jnp
from jax import lax
from jax.sharding import PartitionSpec as P


def layer_norm(rows, gain):
    values = rows.astype(jnp.float32)
    center = jnp.mean(values, axis=-1, keepdims=True)
    spread = jnp.mean(jnp.square(values - center), axis=-1, keepdims=True)
    return ((values - center) * lax.rsqrt(spread + 1e-05) * gain).astype(jnp.bfloat16)


def project_qkv(rows, weight):
    width = rows.shape[3]
    flat = rows.reshape(-1, width)
    full_rows = lax.all_gather(weight.T, "video", axis=1, tiled=True)
    piece = lax.all_gather(full_rows, "frame", axis=0, tiled=True)
    result = lax.dot_general(
        flat, piece, (((1,), (1,)), ((), ())), preferred_element_type=jnp.float32
    )
    return result.astype(jnp.bfloat16).reshape(
        rows.shape[0], rows.shape[1], rows.shape[2], 3 * width
    )


def project_out(rows, weight):

    def apply_cols(piece, start):
        return jnp.dot(rows, piece, preferred_element_type=jnp.float32)

    return apply_cols(lax.all_gather(weight, "video", axis=1, tiled=True), jnp.int32(0))


def project_kv(rows, weight):

    piece = lax.all_gather(weight.T, "frame", axis=0, tiled=True)
    return lax.dot_general(
        rows, piece, (((1,), (1,)), ((), ())), preferred_element_type=jnp.float32
    )


def body(tokens, counts, frame_index, owner_slot, gain_attn, gain_kv, slopes, w_qkv, w_out, w_kv):
    groups = lax.axis_size("frame")
    my_index = lax.axis_index("frame")
    slots_dev = tokens.shape[1]
    patches = tokens.shape[2]
    width = tokens.shape[3]
    n_heads = slopes.shape[0]
    head_size = width // n_heads
    slots_all = slots_dev * groups
    pos_dev = patches // groups
    regrouped = lax.all_to_all(tokens, "frame", split_axis=2, concat_axis=1, tiled=True)
    qkv = project_qkv(layer_norm(regrouped, gain_attn), w_qkv)
    query = qkv[0, :, :, :width].reshape(slots_all, pos_dev, n_heads, head_size)
    keyed = qkv[0, :, :, width : 2 * width].reshape(slots_all, pos_dev, n_heads, head_size)
    valued = qkv[0, :, :, 2 * width :].reshape(slots_all, pos_dev, n_heads, head_size)
    scores = jnp.einsum(
        "sphd,tphd->phst", query, keyed, preferred_element_type=jnp.float32
    ) * head_size ** (-0.5)
    frame_ids = frame_index[0]
    times = frame_ids.astype(jnp.float32)
    distance = jnp.abs(times[:, None] - times[None, :])
    scores = scores - slopes[None, :, None, None] * distance[None, None]
    valid = frame_ids < counts[0]
    scores = jnp.where(valid[None, None, None, :], scores, -1e30)
    top = jnp.max(scores, axis=-1, keepdims=True)
    expo = jnp.exp(scores - top)
    weights = (expo / jnp.sum(expo, axis=-1, keepdims=True)).astype(jnp.bfloat16)
    attended = jnp.einsum("phst,tphd->sphd", weights, valued, preferred_element_type=jnp.float32)
    attended = attended.astype(jnp.bfloat16).reshape(-1, width)
    updated = (
        regrouped.reshape(-1, width).astype(jnp.float32) + project_out(attended, w_out)
    ).astype(jnp.bfloat16)
    updated = updated.reshape(1, slots_all, pos_dev, width)
    inverse = (
        jnp.zeros((slots_all,), jnp.int32)
        .at[owner_slot[0]]
        .set(jnp.arange(slots_all, dtype=jnp.int32))
    )
    outgoing = jnp.take(updated, inverse, axis=1)
    arrived = lax.all_to_all(outgoing, "frame", split_axis=1, concat_axis=2, tiled=True)
    normed_kv = layer_norm(arrived, gain_kv).reshape(-1, width)
    pairs = (
        project_kv(normed_kv, w_kv).astype(jnp.bfloat16).reshape(1, slots_dev, patches, 2 * width)
    )
    sources = lax.dynamic_slice_in_dim(inverse, my_index * slots_dev, slots_dev)
    kept = jnp.take(frame_ids, sources) < counts[0]
    pairs = jnp.where(kept[None, :, None, None], pairs, jnp.zeros_like(pairs))
    return (pairs[..., :width], pairs[..., width:])


def solution(mesh):
    return jax.shard_map(
        body,
        mesh=mesh,
        in_specs=(
            P("video", "frame", None, None),
            P("video"),
            P("video", None),
            P("video", None),
            P(),
            P(),
            P(),
            P("video", "frame"),
            P(None, "video"),
            P(None, "frame"),
        ),
        out_specs=(P("video", "frame", None, None), P("video", "frame", None, None)),
        check_vma=False,
    )
```

```python
import functools
import jax
import jax.numpy as jnp
from jax import lax
from jax.experimental import pallas as pl
from jax.experimental.pallas import tpu as pltpu
from jax.sharding import PartitionSpec as P

XD, YD, ZD = 4, 8, 8
FRAMES = YD * ZD
SLOTS = 2 * FRAMES
POS = 4
ROWS = POS * SLOTS
D = 1024
HEADS = 16
MESH = pl.DeviceIdType.MESH
NT = (((1,), (1,)), ((), ()))
F32 = jnp.float32
BF16 = jnp.bfloat16


def lanes(block):
    return pl.ds(pl.multiple_of(block * 128, 128), 128)


def rows_at(start, count):
    return pl.ds(pl.multiple_of(start, count), count)


def norm(values, gain):
    center = jnp.mean(values, axis=-1, keepdims=True)
    shifted = values - center
    spread = jnp.mean(jnp.square(shifted), axis=-1, keepdims=True)
    return (shifted * lax.rsqrt(spread + 1e-05) * gain).astype(BF16)


def one_hot(rows, row_of_column):
    return jnp.where(rows == row_of_column, 1.0, 0.0).astype(BF16)


def kernel(
    tok, wq_mine, wk_mine, wo_mine, counts, frame_ids, owners, gain1, gain2, slopes,
    keys_out, values_out,
    wq, wk, wo, tx1, rx1, tx2, rx2, held, resid, normed, qkv, attended, updated, bias,
    s_weights, r_weights, s_plane, r_plane, s_tokens, r_tokens,
):
    v = lax.axis_index("video")
    f = lax.axis_index("frame")
    x, c = v // 2, v % 2
    y, z = f // ZD, f % ZD
    x_next, x_prev, x_far = (x + 1) % XD, (x + 3) % XD, (x + 2) % XD
    v_next, v_prev, v_far = 2 * x_next + c, 2 * x_prev + c, 2 * x_far + c
    v_twin = 2 * x + 1 - c

    def remote(src, dst, send, recv, device):
        return pltpu.make_async_remote_copy(
            src_ref=src, dst_ref=dst, send_sem=send, recv_sem=recv,
            device_id=device, device_id_type=MESH,
        )

    def plane_partner(i):
        return ((y + i // ZD) % YD) * ZD + (z + i % ZD) % ZD

    barrier = pltpu.get_barrier_semaphore()

    def greet(i, carry):
        pl.semaphore_signal(barrier, inc=1, device_id=(v, plane_partner(i)), device_id_type=MESH)
        return carry

    lax.fori_loop(1, FRAMES, greet, 0)
    for other in (v_next, v_prev, v_twin):
        pl.semaphore_signal(barrier, inc=1, device_id=(other, f), device_id_type=MESH)

    wq[y, z, :, lanes(v)] = wq_mine[...]
    wk[y, z, :, lanes(v)] = wk_mine[...]
    wo[:, lanes(v)] = wo_mine[...]
    low = lax.broadcasted_iota(jnp.int32, (8, 8, D), 1) < 4

    def lay_out(i, carry):
        first = tok[0, rows_at(64 * i, 64), :].astype(F32).reshape(8, 8, D)
        second = tok[1, rows_at(64 * i, 64), :].astype(F32).reshape(8, 8, D)
        even = jnp.where(low, first, pltpu.roll(second, 4, 1))
        odd = jnp.where(low, pltpu.roll(first, 4, 1), second)
        both = jnp.stack([even, odd], axis=1).reshape(16, 8, D)
        halves = jnp.concatenate([both[:, :, :512], both[:, :, 512:]], axis=1)
        tx1[rows_at(16 * i, 16)] = halves.astype(BF16)
        return carry

    lax.fori_loop(0, 4, lay_out, 0)
    rx1[f] = tx1[f]
    pl.semaphore_wait(barrier, FRAMES - 1 + 3)

    groups = {
        "q": (0, lambda half, block: wq.at[pl.ds(4 * half, 4), :, :, lanes(block)]),
        "o": (1, lambda half, block: wo.at[pl.ds(512 * half, 512), lanes(block)]),
        "k": (2, lambda half, block: wk.at[pl.ds(4 * half, 4), :, :, lanes(block)]),
    }
    moves = [
        (0, v, v_prev, v_next), (1, v, v_prev, v_next),
        (0, v, v_next, v_prev), (1, v, v_next, v_prev),
        (0, v_prev, v_far, v_next), (1, v_next, v_far, v_prev),
        (0, v, v_twin, v_twin), (1, v, v_twin, v_twin),
        (0, v_prev, 2 * x_prev + 1 - c, v_twin), (1, v_prev, 2 * x_prev + 1 - c, v_twin),
        (0, v_next, 2 * x_next + 1 - c, v_twin), (1, v_next, 2 * x_next + 1 - c, v_twin),
        (0, v_far, 2 * x_far + 1 - c, v_twin), (1, v_far, 2 * x_far + 1 - c, v_twin),
    ]

    def move(name, number):
        group, view = groups[name]
        half, block, _, target = moves[number]
        return remote(
            view(half, block), view(half, block),
            s_weights.at[group, number], r_weights.at[group, number], (target, f),
        )

    def start(name, *numbers):
        for number in numbers:
            move(name, number).start()

    def arrive(name, *numbers):
        group, view = groups[name]
        for number in numbers:
            half, _, block, target = moves[number]
            remote(
                view(half, block), view(half, block),
                s_weights.at[group, number], r_weights.at[group, number], (target, f),
            ).wait_recv()

    def own_moves(name):
        start(name, 0, 3, 1, 2, 6, 7)

    def forward_moves(name):
        arrive(name, 0)
        start(name, 4, 8)
        arrive(name, 3)
        start(name, 5, 11)
        arrive(name, 1)
        start(name, 9)
        arrive(name, 2)
        start(name, 10)

    def far_moves(name):
        arrive(name, 4)
        start(name, 12)
        arrive(name, 5)
        start(name, 13)

    def twin_moves(name):
        arrive(name, *range(6, 14))

    def plane_z(ref, mine, number):
        def send(i, carry):
            here = ref.at[y, z, :, lanes(v)]
            remote(mine, here, s_plane.at[number], r_plane.at[number],
                   (v, y * ZD + (z + i) % ZD)).start()
            return carry
        lax.fori_loop(1, ZD, send, 0)

    def plane_z_wait(ref, number):
        span = ref.at[0, pl.ds(0, ZD - 1), :, lanes(v)]
        remote(span, span, s_plane.at[number], r_plane.at[number], (v, f)).wait_recv()

    def plane_y(ref, number):
        def send(i, carry):
            here = ref.at[y, :, :, lanes(v)]
            remote(here, here, s_plane.at[number], r_plane.at[number],
                   (v, ((y + i) % YD) * ZD + z)).start()
            return carry
        lax.fori_loop(1, YD, send, 0)

    def plane_y_wait(ref, number):
        span = ref.at[pl.ds(0, YD - 1), :, :, lanes(v)]
        remote(span, span, s_plane.at[number], r_plane.at[number], (v, f)).wait_recv()

    def exchange(src, dst, number):
        def send(i, carry):
            g = plane_partner(i)
            remote(src.at[g], dst.at[f], s_tokens.at[number], r_tokens.at[number], (v, g)).start()
            return carry
        lax.fori_loop(1, FRAMES, send, 0)

    def exchange_wait(dst, number):
        span = dst.at[pl.ds(0, FRAMES - 1)]
        remote(span, span, s_tokens.at[number], r_tokens.at[number], (v, f)).wait_recv()

    own_moves("o")
    plane_z(wq, wq_mine, 0)
    plane_z(wk, wk_mine, 2)
    plane_z_wait(wq, 0)
    plane_y(wq, 1)
    exchange(tx1, rx1, 0)
    plane_y_wait(wq, 1)
    own_moves("q")
    plane_z_wait(wk, 2)
    plane_y(wk, 3)
    forward_moves("o")
    far_moves("o")
    forward_moves("q")

    slot_row = owners[...]
    frame_row = frame_ids[...].astype(F32)
    sub = lax.broadcasted_iota(jnp.int32, (SLOTS, SLOTS), 0)
    lane = lax.broadcasted_iota(jnp.int32, (SLOTS, SLOTS), 1)
    place = jnp.where(sub == slot_row, 1.0, 0.0)
    time_col = jnp.sum(place * frame_row, axis=1, keepdims=True)
    time_row = jnp.sum(jnp.where(sub == lane, time_col, 0.0), axis=0, keepdims=True)
    count = counts[0].astype(F32)
    distance = jnp.abs(time_col - time_row)
    valid = time_row < count

    def head_bias(h, carry):
        bias[h] = jnp.where(valid, -slopes[h] * distance, -1e30)
        return carry

    lax.fori_loop(0, HEADS, head_bias, 0)
    row_pos = lax.broadcasted_iota(jnp.int32, (SLOTS, ROWS), 1)
    spread = jnp.where(
        row_pos // POS == lax.broadcasted_iota(jnp.int32, (SLOTS, ROWS), 0), 1.0, 0.0
    )
    slot_col = jnp.sum(
        jnp.where(sub == lane, slot_row.astype(F32), 0.0), axis=1, keepdims=True
    )
    target = jnp.sum(spread * slot_col, axis=0, keepdims=True).astype(jnp.int32)
    target = target + (lax.broadcasted_iota(jnp.int32, (1, ROWS), 1) % POS) * SLOTS

    exchange_wait(rx1, 0)

    def unpack(i, carry):
        blocks = rx1[rows_at(8 * i, 8)].astype(F32)
        held[rows_at(64 * i, 64), :512] = blocks[:, :8].reshape(64, 512).astype(BF16)
        held[rows_at(64 * i, 64), 512:] = blocks[:, 8:].reshape(64, 512).astype(BF16)
        return carry

    lax.fori_loop(0, 8, unpack, 0)
    out_row = lax.broadcasted_iota(jnp.int32, (SLOTS, ROWS), 0)

    def place_and_norm(p, carry):
        picked = jnp.dot(
            one_hot(out_row + p * SLOTS, target), held[...], preferred_element_type=F32
        )
        resid[rows_at(SLOTS * p, SLOTS)] = picked.astype(BF16)
        normed[rows_at(SLOTS * p, SLOTS)] = norm(picked, gain1[...])
        return carry

    lax.fori_loop(0, POS, place_and_norm, 0)

    far_moves("q")
    plane_y_wait(wk, 3)
    own_moves("k")
    twin_moves("q")

    def project(j, carry):
        weight = wq[rows_at(2 * j, 2)].reshape(768, D)
        result = lax.dot_general(normed[...], weight, NT, preferred_element_type=F32)
        qkv[:, pl.ds(pl.multiple_of(768 * j, 128), 768)] = result.astype(BF16)
        return carry

    lax.fori_loop(0, 4, project, 0)
    forward_moves("k")

    left = lax.broadcasted_iota(jnp.int32, (SLOTS, 128), 1) < 64

    def attend(i, carry):
        p = i // 4
        here = rows_at(SLOTS * p, SLOTS)
        for j in range(2):
            pair = (i % 4) * 2 + j
            query = qkv[here, lanes(pair)]
            keyed = qkv[here, lanes(8 + pair)]
            valued = qkv[here, lanes(16 + pair)]
            parts = []
            for side in range(2):
                mine = left if side == 0 else jnp.logical_not(left)
                scores = lax.dot_general(
                    jnp.where(mine, query, jnp.zeros_like(query)), keyed, NT,
                    preferred_element_type=F32,
                )
                scores = scores * 0.125 + bias[2 * pair + side]
                expo = jnp.exp(scores - jnp.max(scores, axis=1, keepdims=True))
                weights = expo * (1.0 / jnp.sum(expo, axis=1, keepdims=True))
                parts.append(
                    jnp.dot(weights.astype(BF16), valued, preferred_element_type=F32)
                )
            attended[here, lanes(pair)] = jnp.where(left, parts[0], parts[1]).astype(BF16)
        return carry

    lax.fori_loop(0, 16, attend, 0)
    twin_moves("o")

    def project_out(p, carry):
        here = rows_at(SLOTS * p, SLOTS)
        added = jnp.dot(attended[here], wo[...], preferred_element_type=F32)
        updated[here] = (resid[here].astype(F32) + added).astype(BF16)
        return carry

    lax.fori_loop(0, POS, project_out, 0)

    out_col = lax.broadcasted_iota(jnp.int32, (128, ROWS), 1)
    out_row2 = lax.broadcasted_iota(jnp.int32, (128, ROWS), 0)

    def lay_out_updated(i, carry):
        row = out_row2 + 128 * i
        source = (row % 4) * SLOTS + 2 * (row // 8) + (row % 8) // 4
        moved = jnp.dot(one_hot(source, out_col), updated[...], preferred_element_type=F32)
        both = moved.reshape(16, 8, D)
        halves = jnp.concatenate([both[:, :, :512], both[:, :, 512:]], axis=1)
        tx2[rows_at(16 * i, 16)] = halves.astype(BF16)
        return carry

    lax.fori_loop(0, 4, lay_out_updated, 0)
    exchange(tx2, rx2, 1)
    rx2[f] = tx2[f]
    far_moves("k")
    twin_moves("k")
    exchange_wait(rx2, 1)

    def norm_arrived(i, carry):
        blocks = rx2[rows_at(16 * i, 16)].astype(F32)
        both = jnp.concatenate([blocks[:, :8], blocks[:, 8:]], axis=2).reshape(8, 2, 8, D)
        even, odd = both[:, 0], both[:, 1]
        first = jnp.where(low, even, pltpu.roll(odd, 4, 1)).reshape(64, D)
        second = jnp.where(low, pltpu.roll(even, 4, 1), odd).reshape(64, D)
        normed[rows_at(64 * i, 64)] = norm(first, gain2[...])
        normed[rows_at(256 + 64 * i, 64)] = norm(second, gain2[...])
        return carry

    lax.fori_loop(0, 4, norm_arrived, 0)

    lane_row = lax.broadcasted_iota(jnp.int32, (1, SLOTS), 1)
    kept = jnp.where(valid, 1.0, 0.0)
    kept_first = jnp.sum(jnp.where(lane_row == 2 * f, kept, 0.0), axis=1, keepdims=True)
    kept_second = jnp.sum(jnp.where(lane_row == 2 * f + 1, kept, 0.0), axis=1, keepdims=True)
    row_kept = jnp.where(
        lax.broadcasted_iota(jnp.int32, (ROWS, 1), 0) < 256, kept_first, kept_second
    ) > 0.5

    for j in range(4):
        weight = wk[pl.ds(2 * j, 2)].reshape(512, D)
        result = lax.dot_general(normed[...], weight, NT, preferred_element_type=F32)
        result = jnp.where(row_kept, result, 0.0).astype(BF16)
        out = keys_out if j < 2 else values_out
        out[:, pl.ds(512 * (j % 2), 512)] = result

    for name in groups:
        for number in range(len(moves)):
            move(name, number).wait_send()
    for number, ref in ((0, wq), (2, wk)):
        span = ref.at[0, pl.ds(0, ZD - 1), :, lanes(v)]
        remote(span, span, s_plane.at[number], r_plane.at[number], (v, f)).wait_send()
    for number, ref in ((1, wq), (3, wk)):
        span = ref.at[pl.ds(0, YD - 1), :, :, lanes(v)]
        remote(span, span, s_plane.at[number], r_plane.at[number], (v, f)).wait_send()
    for number, ref in ((0, rx1), (1, rx2)):
        span = ref.at[pl.ds(0, FRAMES - 1)]
        remote(span, span, s_tokens.at[number], r_tokens.at[number], (v, f)).wait_send()


def body(tokens, counts, frame_index, owner_slot, gain_attn, gain_kv, slopes, w_qkv, w_out, w_kv):
    v = lax.axis_index("video")
    wq_mine = w_qkv.T
    wk_mine = lax.dynamic_slice_in_dim(w_kv, v * 128, 128, 0).T
    vmem = pl.BlockSpec(memory_space=pltpu.VMEM)
    smem = pl.BlockSpec(memory_space=pltpu.SMEM)
    dma = pltpu.SemaphoreType.DMA
    keys, values = pl.pallas_call(
        kernel,
        out_shape=(
            jax.ShapeDtypeStruct((ROWS, D), BF16),
            jax.ShapeDtypeStruct((ROWS, D), BF16),
        ),
        in_specs=[vmem] * 4 + [smem] + [vmem] * 4 + [smem],
        out_specs=(vmem, vmem),
        scratch_shapes=[
            pltpu.VMEM((YD, ZD, 48, D), BF16),
            pltpu.VMEM((YD, ZD, 32, D), BF16),
            pltpu.VMEM((D, D), BF16),
            pltpu.VMEM((FRAMES, 16, 512), BF16),
            pltpu.VMEM((FRAMES, 16, 512), BF16),
            pltpu.VMEM((FRAMES, 16, 512), BF16),
            pltpu.VMEM((FRAMES, 16, 512), BF16),
            pltpu.VMEM((ROWS, D), BF16),
            pltpu.VMEM((ROWS, D), BF16),
            pltpu.VMEM((ROWS, D), BF16),
            pltpu.VMEM((ROWS, 3 * D), BF16),
            pltpu.VMEM((ROWS, D), BF16),
            pltpu.VMEM((ROWS, D), BF16),
            pltpu.VMEM((HEADS, SLOTS, SLOTS), F32),
            dma((3, 14)), dma((3, 14)), dma((4,)), dma((4,)), dma((2,)), dma((2,)),
        ],
        compiler_params=pltpu.CompilerParams(
            collective_id=0, has_side_effects=True, vmem_limit_bytes=60 * 2**20
        ),
    )(
        tokens[0], wq_mine, wk_mine, w_out, counts, frame_index, owner_slot,
        gain_attn.reshape(1, D), gain_kv.reshape(1, D), slopes,
    )
    return keys.reshape(1, 2, 256, D), values.reshape(1, 2, 256, D)


def solution(mesh):
    return jax.shard_map(
        body,
        mesh=mesh,
        in_specs=(
            P("video", "frame", None, None),
            P("video"),
            P("video", None),
            P("video", None),
            P(),
            P(),
            P(),
            P("video", "frame"),
            P(None, "video"),
            P(None, "frame"),
        ),
        out_specs=(P("video", "frame", None, None), P("video", "frame", None, None)),
        check_vma=False,
    )
```

```python
import functools
import jax
import jax.numpy as jnp
from jax import lax
from jax.experimental import pallas as pl
from jax.experimental.pallas import tpu as pltpu
from jax.sharding import PartitionSpec as P

XD, YD, ZD = 4, 8, 8
FRAMES = YD * ZD
SLOTS = 2 * FRAMES
POS = 4
ROWS = POS * SLOTS
D = 1024
HEADS = 16
NEAR = (1, 7, 2, 6, 3, 5, 4)
MESH = pl.DeviceIdType.MESH
NT = (((1,), (1,)), ((), ()))
F32 = jnp.float32
BF16 = jnp.bfloat16


def lanes(block):
    return pl.ds(pl.multiple_of(block * 128, 128), 128)


def rows_at(start, count):
    return pl.ds(pl.multiple_of(start, count), count)


def norm(values, gain):
    center = jnp.mean(values, axis=-1, keepdims=True)
    shifted = values - center
    spread = jnp.mean(jnp.square(shifted), axis=-1, keepdims=True)
    return (shifted * lax.rsqrt(spread + 1e-05) * gain).astype(BF16)


def one_hot(rows, row_of_column):
    return jnp.where(rows == row_of_column, 1.0, 0.0).astype(BF16)


def kernel(
    tok, wq_mine, wk_mine, wo_mine, counts, frame_ids, owners, gain1, gain2, slopes,
    keys_out, values_out,
    wq, wk, wo, tx1, rx1, tx2, rx2, held, resid, normed, query_t, keyed, value_t,
    attended_t, bias, own_q, own_k,
    s_plane, r_plane, r_piece, s_span, r_span, s_tokens, r_tokens, row_in,
):
    v = lax.axis_index("video")
    f = lax.axis_index("frame")
    x, c = v // 2, v % 2
    y, z = f // ZD, f % ZD
    x_next, x_prev, x_far = (x + 1) % XD, (x + 3) % XD, (x + 2) % XD
    v_next, v_prev, v_far = 2 * x_next + c, 2 * x_prev + c, 2 * x_far + c
    v_twin = 2 * x + 1 - c

    def remote(src, dst, send, recv, device):
        return pltpu.make_async_remote_copy(
            src_ref=src, dst_ref=dst, send_sem=send, recv_sem=recv,
            device_id=device, device_id_type=MESH,
        )

    def along_y(i):
        return (v, ((y + i) % YD) * ZD + z)

    def along_z(i):
        return (v, y * ZD + (z + i) % ZD)

    barrier = pltpu.get_barrier_semaphore()
    for i in range(1, 8):
        for device in (along_y(i), along_z(i)):
            pl.semaphore_signal(barrier, inc=1, device_id=device, device_id_type=MESH)
    for other in (v_next, v_prev, v_twin):
        pl.semaphore_signal(barrier, inc=1, device_id=(other, f), device_id_type=MESH)

    own_q[...] = wq_mine[...]
    own_k[...] = wk_mine[:, lanes(v)]
    wq[y, z, :, lanes(v)] = own_q[...]
    wk[y, z, :, lanes(v)] = own_k[...]
    wo[:, lanes(v)] = wo_mine[...]
    low = lax.broadcasted_iota(jnp.int32, (8, 8, D), 1) < 4

    def lay_out(i, carry):
        first = tok[0, rows_at(64 * i, 64), :].astype(F32).reshape(8, 8, D)
        second = tok[1, rows_at(64 * i, 64), :].astype(F32).reshape(8, 8, D)
        even = jnp.where(low, first, pltpu.roll(second, 4, 1))
        odd = jnp.where(low, pltpu.roll(first, 4, 1), second)
        both = jnp.stack([even, odd], axis=1).reshape(16, 8, D)
        halves = jnp.concatenate([both[:, :, :512], both[:, :, 512:]], axis=1)
        tx1[rows_at(16 * i, 16)] = halves.astype(BF16)
        return carry

    lax.fori_loop(0, 4, lay_out, 0)
    rx1[f] = tx1[f]
    pl.semaphore_wait(barrier, 17)
    for i in NEAR:
        pl.semaphore_signal(row_in, inc=1, device_id=along_y(i), device_id_type=MESH)

    def q_piece(core, i, block):
        if core == 0:
            return wq.at[(y + i) % YD, :, :, lanes(block)]
        return wq.at[:, (z + i) % ZD, :, lanes(block)]

    def whole(ref, block):
        return ref.at[:, lanes(block)] if ref is wo else ref.at[:, :, :, lanes(block)]

    def half(ref, number, block):
        if ref is wo:
            return wo.at[pl.ds(512 * number, 512), lanes(block)]
        return ref.at[pl.ds(4 * number, 4), :, :, lanes(block)]

    def plane_first(core, ref, mine, number):
        here = ref.at[y, z, :, lanes(v)]
        for i in NEAR:
            remote(mine, here, s_plane.at[number], r_plane.at[number],
                   along_z(i) if core == 0 else along_y(i)).start()

    def seven(core, ref):
        if core == 0:
            return ref.at[0, pl.ds(0, 7), :, lanes(v)]
        return ref.at[pl.ds(0, 7), 0, :, lanes(v)]

    def plane_first_wait(core, ref, number):
        span = seven(core, ref)
        remote(span, span, s_plane.at[number], r_plane.at[number], (v, f)).wait_recv()

    def send_tokens(src, dst, number, to_y, to_z):
        g = to_y * ZD + to_z
        remote(src.at[g], dst.at[f], s_tokens.at[number], r_tokens.at[number], (v, g)).start()

    def tokens_wait(dst, number):
        span = dst.at[pl.ds(0, FRAMES - 1)]
        remote(span, span, s_tokens.at[number], r_tokens.at[number], (v, f)).wait_recv()

    groups = {"q": (0, wq), "o": (1, wo), "k": (2, wk)}
    moves = [
        (0, v, v_prev, v_next), (1, v, v_prev, v_next),
        (0, v, v_next, v_prev), (1, v, v_next, v_prev),
        (0, v_prev, v_far, v_next), (1, v_next, v_far, v_prev),
        (None, v, v_twin, v_twin),
        (None, v_prev, 2 * x_prev + 1 - c, v_twin),
        (None, v_next, 2 * x_next + 1 - c, v_twin),
        (0, v_far, 2 * x_far + 1 - c, v_twin), (1, v_far, 2 * x_far + 1 - c, v_twin),
    ]

    def view(name, part, block):
        ref = groups[name][1]
        return whole(ref, block) if part is None else half(ref, part, block)

    def move(name, number):
        group = groups[name][0]
        part, block, _, target = moves[number]
        here = view(name, part, block)
        return remote(here, here, s_span.at[group, number], r_span.at[group, number], (target, f))

    def start(name, *numbers):
        for number in numbers:
            move(name, number).start()

    def arrive(name, *numbers):
        group = groups[name][0]
        for number in numbers:
            part, _, block, target = moves[number]
            here = view(name, part, block)
            remote(
                here, here, s_span.at[group, number], r_span.at[group, number], (target, f)
            ).wait_recv()

    def own_moves(name):
        start(name, 0, 3, 1, 2, 6)

    def forward_moves(name):
        arrive(name, 0)
        start(name, 4)
        arrive(name, 3)
        start(name, 5)
        arrive(name, 1)
        start(name, 7)
        arrive(name, 2)
        start(name, 8)

    def far_moves(name):
        arrive(name, 4)
        start(name, 9)
        arrive(name, 5)
        start(name, 10)

    def twin_moves(name):
        arrive(name, 6, 7, 8, 9, 10)

    def gather(core):
        order = (0,) + NEAR
        plane_first(core, wq, own_q, 0)
        plane_first(core, wk, own_k, 1)
        own_moves("o")
        plane_first_wait(core, wq, 0)

        def send_x(position):
            i = -order[position] % 8
            here = q_piece(core, i, v)
            remote(here, here, s_span.at[0, 0], r_piece.at[1, position], (v_next, f)).start()
            remote(here, here, s_span.at[0, 1], r_piece.at[2, position], (v_prev, f)).start()

        def arrived(column, position, block):
            here = q_piece(core, -order[position] % 8, block)
            remote(here, here, s_span.at[0, 0], r_piece.at[column, position], (v, f)).wait_recv()

        def forward(position):
            arrived(1, position, v_prev)
            if position % 2 == 0:
                here = q_piece(core, -order[position] % 8, v_prev)
                remote(here, here, s_span.at[0, 2], r_piece.at[3, position], (v_next, f)).start()
            arrived(2, position, v_next)
            if position % 2 == 1:
                here = q_piece(core, -order[position] % 8, v_next)
                remote(here, here, s_span.at[0, 2], r_piece.at[3, position], (v_prev, f)).start()

        step = along_y if core == 0 else along_z

        def hand_on(position):
            i = order[position]
            here = q_piece(core, -i % 8, v)
            if position == 0:
                onward = ((1, 1, 2), (7, 2, 4))
            elif i < 4:
                onward = ((1, position + 2 if i < 3 else 7, 2),)
            elif i > 5:
                onward = ((7, position + 2, 4),)
            else:
                onward = ()
            for towards, place, number in onward:
                remote(here, here, s_plane.at[number], r_piece.at[0, place], step(towards)).start()

        def some_tokens(part):
            for k in range(1 + part, FRAMES, 8):
                other = 29 * k % FRAMES
                send_tokens(tx1, rx1, 0, (y + other // ZD) % YD, (z + other % ZD) % ZD)

        hand_on(0)
        send_x(0)
        pl.semaphore_wait(row_in, 7)
        some_tokens(0)
        for position in range(1, 8):
            some_tokens(position)
            arrived(0, position, v)
            hand_on(position)
            send_x(position)
            if position >= 3:
                forward(position - 3)
        start("q", 6)
        plane_first_wait(core, wk, 1)
        for position in range(5, 8):
            forward(position)
        start("q", 7, 8)
        for position in range(8):
            arrived(3, position, v_far)
            here = q_piece(core, -order[position] % 8, v_far)
            remote(here, here, s_span.at[0, 3], r_piece.at[4, position], (v_twin, f)).start()
        forward_moves("o")
        far_moves("o")

    @pl.when(c == 0)
    def _():
        gather(0)

    @pl.when(c == 1)
    def _():
        gather(1)

    slot_row = owners[...]
    frame_row = frame_ids[...].astype(F32)
    sub = lax.broadcasted_iota(jnp.int32, (SLOTS, SLOTS), 0)
    lane = lax.broadcasted_iota(jnp.int32, (SLOTS, SLOTS), 1)
    place = jnp.where(sub == slot_row, 1.0, 0.0)
    time_col = jnp.sum(place * frame_row, axis=1, keepdims=True)
    time_row = jnp.sum(jnp.where(sub == lane, time_col, 0.0), axis=0, keepdims=True)
    count = counts[0].astype(F32)
    distance = jnp.abs(time_col - time_row)
    valid_col = time_col < count

    for h in range(HEADS):
        bias[h // 2, :, 128 * (h % 2) : 128 * (h % 2) + 128] = jnp.where(
            valid_col, -slopes[h] * distance, -1e30
        )
    row_slot = lax.broadcasted_iota(jnp.int32, (SLOTS, ROWS), 1) // POS
    slot_col = jnp.sum(
        jnp.where(sub == lane, slot_row.astype(F32), 0.0), axis=1, keepdims=True
    )
    owner = jnp.sum(
        jnp.where(row_slot == lax.broadcasted_iota(jnp.int32, (SLOTS, ROWS), 0), slot_col, 0.0),
        axis=0, keepdims=True,
    ).astype(jnp.int32)
    row_pos = lax.broadcasted_iota(jnp.int32, (1, ROWS), 1) % POS
    to_attend = row_pos * SLOTS + owner
    to_send = owner * POS + row_pos
    out_row = lax.broadcasted_iota(jnp.int32, (128, ROWS), 0)

    tokens_wait(rx1, 0)

    def k_plane(core):
        mine_k = wk.at[y, :, :, lanes(v)] if core == 0 else wk.at[:, z, :, lanes(v)]
        for i in NEAR:
            remote(mine_k, mine_k, s_plane.at[3], r_plane.at[3],
                   along_y(i) if core == 0 else along_z(i)).start()

    @pl.when(c == 0)
    def _():
        k_plane(0)

    @pl.when(c == 1)
    def _():
        k_plane(1)

    def unpack(i, carry):
        blocks = rx1[rows_at(8 * i, 8)].astype(F32)
        held[rows_at(64 * i, 64), :512] = blocks[:, :8].reshape(64, 512).astype(BF16)
        held[rows_at(64 * i, 64), 512:] = blocks[:, 8:].reshape(64, 512).astype(BF16)
        return carry

    lax.fori_loop(0, 8, unpack, 0)

    def place_and_norm(p, carry):
        here = rows_at(128 * p, 128)
        picked = jnp.dot(
            one_hot(out_row + p * 128, to_attend), held[...], preferred_element_type=F32
        )
        normed[here] = norm(picked, gain1[...])
        resid[here] = jnp.dot(
            one_hot(out_row + p * 128, to_send), held[...], preferred_element_type=F32
        ).astype(BF16)
        return carry

    lax.fori_loop(0, POS, place_and_norm, 0)

    for position in range(8):
        here = wq.at[0, :, :, lanes(v_twin)]
        remote(here, here, s_span.at[0, 3], r_piece.at[4, position], (v_twin, f)).wait_recv()
    arrive("q", 6, 7, 8)

    flat = wq.reshape(3 * D, D)

    def project(j, carry):
        here = rows_at(512 * j, 512)
        query = lax.dot_general(flat[here], normed[...], NT, preferred_element_type=F32)
        query_t[here] = (query.astype(BF16) * 0.125).astype(BF16)
        value = lax.dot_general(
            flat[pl.ds(pl.multiple_of(2048 + 512 * j, 512), 512)], normed[...], NT,
            preferred_element_type=F32,
        )
        value_t[here] = value.astype(BF16)
        key = lax.dot_general(
            normed[...], flat[pl.ds(pl.multiple_of(1024 + 512 * j, 512), 512)], NT,
            preferred_element_type=F32,
        )
        keyed[:, rows_at(512 * j, 512)] = key.astype(BF16)
        return carry

    lax.fori_loop(0, 2, project, 0)
    span = wk.at[pl.ds(0, 7), :, :, lanes(v)]
    remote(span, span, s_plane.at[3], r_plane.at[3], (v, f)).wait_recv()
    own_moves("k")

    blank = jnp.zeros((64, 128), BF16)
    ones = jnp.ones((16, 128), BF16)

    def attend(p, carry):
        here = rows_at(SLOTS * p, SLOTS)
        for pair in range(8):
            top, bottom = pl.ds(128 * pair, 64), pl.ds(128 * pair + 64, 64)
            queries = jnp.concatenate([
                jnp.concatenate([query_t[top, here], blank], axis=1),
                jnp.concatenate([blank, query_t[bottom, here]], axis=1),
            ], axis=0)
            scores = jnp.dot(
                keyed[here, 128 * pair : 128 * pair + 128], queries, preferred_element_type=F32
            ) + bias[pair]
            expo = jnp.exp(scores - jnp.max(scores, axis=0, keepdims=True)).astype(BF16)
            values = jnp.concatenate([value_t[pl.ds(128 * pair, 128), here], ones], axis=0)
            summed = jnp.dot(values, expo, preferred_element_type=F32)
            scale = 1.0 / summed[128:129]
            attended_t[top, here] = (summed[:64, :128] * scale[:, :128]).astype(BF16)
            attended_t[bottom, here] = (summed[64:128, 128:] * scale[:, 128:]).astype(BF16)
        return carry

    lax.fori_loop(0, POS, attend, 0)
    twin_moves("o")

    column = lax.broadcasted_iota(jnp.int32, (1, ROWS), 1)
    from_attend = (column % SLOTS) * POS + column // SLOTS

    for i in range(4):
        quarter = (y // 2 + i) % 4
        here = rows_at(128 * quarter, 128)
        moved = lax.dot_general(
            one_hot(out_row + 128 * quarter, from_attend), attended_t[...], NT,
            preferred_element_type=F32,
        ).astype(BF16)
        added = jnp.dot(moved, wo[...], preferred_element_type=F32)
        both = (resid[here].astype(F32) + added).reshape(16, 8, D)
        halves = jnp.concatenate([both[:, :, :512], both[:, :, 512:]], axis=1)
        tx2[rows_at(16 * quarter, 16)] = halves.astype(BF16)
        for k in range(8):
            to_z = (z + k) % ZD
            if i == 0:
                if k:
                    send_tokens(tx2, rx2, 1, y, to_z)
                send_tokens(tx2, rx2, 1, y // 2 * 2 + 1 - y % 2, to_z)
            else:
                send_tokens(tx2, rx2, 1, 2 * quarter, to_z)
                send_tokens(tx2, rx2, 1, 2 * quarter + 1, to_z)

    rx2[f] = tx2[f]
    forward_moves("k")
    far_moves("k")
    twin_moves("k")
    tokens_wait(rx2, 1)

    def norm_arrived(i, carry):
        blocks = rx2[rows_at(16 * i, 16)].astype(F32)
        both = jnp.concatenate([blocks[:, :8], blocks[:, 8:]], axis=2).reshape(8, 2, 8, D)
        even, odd = both[:, 0], both[:, 1]
        first = jnp.where(low, even, pltpu.roll(odd, 4, 1)).reshape(64, D)
        second = jnp.where(low, pltpu.roll(even, 4, 1), odd).reshape(64, D)
        normed[rows_at(64 * i, 64)] = norm(first, gain2[...])
        normed[rows_at(256 + 64 * i, 64)] = norm(second, gain2[...])
        return carry

    lax.fori_loop(0, 4, norm_arrived, 0)

    kept = jnp.where(valid_col, 1.0, 0.0)
    slot_sub = lax.broadcasted_iota(jnp.int32, (SLOTS, 1), 0)
    kept_first = jnp.sum(jnp.where(slot_sub == 2 * f, kept, 0.0), axis=0, keepdims=True)
    kept_second = jnp.sum(jnp.where(slot_sub == 2 * f + 1, kept, 0.0), axis=0, keepdims=True)
    row_kept = jnp.where(
        lax.broadcasted_iota(jnp.int32, (ROWS, 1), 0) < 256, kept_first, kept_second
    ) > 0.5

    for j in range(4):
        weight = wk[pl.ds(2 * j, 2)].reshape(512, D)
        result = lax.dot_general(normed[...], weight, NT, preferred_element_type=F32)
        result = jnp.where(row_kept, result, 0.0).astype(BF16)
        out = keys_out if j < 2 else values_out
        out[:, pl.ds(512 * (j % 2), 512)] = result

    def sent(span, semaphore):
        remote(span, span, semaphore, r_plane.at[0], (v, f)).wait_send()

    for name, numbers in (("q", (6, 7, 8)), ("o", range(11)), ("k", range(11))):
        for number in numbers:
            move(name, number).wait_send()
    for number in range(4):
        sent(whole(wq, v), s_span.at[0, number])
    sent(wq.at[0, pl.ds(0, 7), :, lanes(v)], s_plane.at[0])
    sent(wk.at[0, pl.ds(0, 7), :, lanes(v)], s_plane.at[1])
    sent(wq.at[pl.ds(0, 4), :, :, lanes(v)], s_plane.at[2])
    sent(wq.at[pl.ds(0, 3), :, :, lanes(v)], s_plane.at[4])
    sent(wk.at[pl.ds(0, 7), :, :, lanes(v)], s_plane.at[3])
    for number in range(2):
        sent(rx1.at[pl.ds(0, FRAMES - 1)], s_tokens.at[number])


def body(tokens, counts, frame_index, owner_slot, gain_attn, gain_kv, slopes, w_qkv, w_out, w_kv):
    vmem = pl.BlockSpec(memory_space=pltpu.VMEM)
    smem = pl.BlockSpec(memory_space=pltpu.SMEM)
    dma = pltpu.SemaphoreType.DMA
    keys, values = pl.pallas_call(
        kernel,
        out_shape=(
            jax.ShapeDtypeStruct((ROWS, D), BF16),
            jax.ShapeDtypeStruct((ROWS, D), BF16),
        ),
        in_specs=[vmem] * 4 + [smem] + [vmem] * 4 + [smem],
        out_specs=(vmem, vmem),
        scratch_shapes=[
            pltpu.VMEM((YD, ZD, 48, D), BF16),
            pltpu.VMEM((YD, ZD, 32, D), BF16),
            pltpu.VMEM((D, D), BF16),
            *[pltpu.VMEM((FRAMES, 16, 512), BF16) for _ in range(4)],
            pltpu.VMEM((ROWS, D), BF16),
            pltpu.VMEM((ROWS, D), BF16),
            pltpu.VMEM((ROWS, D), BF16),
            pltpu.VMEM((D, ROWS), BF16),
            pltpu.VMEM((ROWS, D), BF16),
            pltpu.VMEM((D, ROWS), BF16),
            pltpu.VMEM((D, ROWS), BF16),
            pltpu.VMEM((8, SLOTS, 256), F32),
            pltpu.VMEM((48, 128), BF16),
            pltpu.VMEM((32, 128), BF16),
            dma((5,)), dma((4,)), dma((5, 8)), dma((3, 11)), dma((3, 11)), dma((2,)), dma((2,)),
            pltpu.SemaphoreType.REGULAR,
        ],
        compiler_params=pltpu.CompilerParams(
            collective_id=0, has_side_effects=True, vmem_limit_bytes=60 * 2**20
        ),
    )(
        tokens[0], w_qkv.T, w_kv.T, w_out, counts, frame_index, owner_slot,
        gain_attn.reshape(1, D), gain_kv.reshape(1, D), slopes,
    )
    return keys.reshape(1, 2, 256, D), values.reshape(1, 2, 256, D)


def solution(mesh):
    return jax.shard_map(
        body,
        mesh=mesh,
        in_specs=(
            P("video", "frame", None, None),
            P("video"),
            P("video", None),
            P("video", None),
            P(),
            P(),
            P(),
            P("video", "frame"),
            P(None, "video"),
            P(None, "frame"),
        ),
        out_specs=(P("video", "frame", None, None), P("video", "frame", None, None)),
        check_vma=False,
    )
```

```python
import functools
import jax
import jax.numpy as jnp
from jax import lax
from jax.experimental import pallas as pl
from jax.experimental.pallas import tpu as pltpu
from jax.sharding import PartitionSpec as P

XD, YD, ZD = 4, 8, 8
FRAMES = YD * ZD
SLOTS = 2 * FRAMES
POS = 4
ROWS = POS * SLOTS
D = 1024
HEADS = 16
NEAR = (1, 7, 2, 6, 3, 5, 4)
STEPS = sorted(
    range(1, FRAMES), key=lambda k: min(k // ZD, YD - k // ZD) + min(k % ZD, ZD - k % ZD)
)
TURNS = [k for pair in zip(STEPS[::-1], STEPS) for k in pair][: FRAMES - 1]
VMEM_MIB = 60
MESH = pl.DeviceIdType.MESH
NT = (((1,), (1,)), ((), ()))
F32 = jnp.float32
BF16 = jnp.bfloat16


def lanes(block):
    return pl.ds(pl.multiple_of(block * 128, 128), 128)


def rows_at(start, count):
    return pl.ds(pl.multiple_of(start, count), count)


def norm(values, gain):
    center = jnp.mean(values, axis=-1, keepdims=True)
    shifted = values - center
    spread = jnp.mean(jnp.square(shifted), axis=-1, keepdims=True)
    return (shifted * lax.rsqrt(spread + 1e-05) * gain).astype(BF16)


def one_hot(rows, row_of_column):
    return jnp.where(rows == row_of_column, 1.0, 0.0).astype(BF16)


def kernel(
    tok, wq_mine, wk_mine, wo_mine, counts, frame_ids, owners, gain1, gain2, slopes,
    keys_out, values_out,
    wq, wk, wo, tx1, rx1, tx2, rx2, held, resid, normed, query_t, keyed, value_t,
    attended_t, bias, own_q, own_k, part_q, part_k, part_v,
    s_plane, r_plane, r_piece, s_span, r_span, s_tokens, r_tokens, r_quarter, row_in,
):
    v = lax.axis_index("video")
    f = lax.axis_index("frame")
    x, c = v // 2, v % 2
    y, z = f // ZD, f % ZD
    x_next, x_prev, x_far = (x + 1) % XD, (x + 3) % XD, (x + 2) % XD
    v_next, v_prev, v_far = 2 * x_next + c, 2 * x_prev + c, 2 * x_far + c
    v_twin = 2 * x + 1 - c

    def remote(src, dst, send, recv, device):
        return pltpu.make_async_remote_copy(
            src_ref=src, dst_ref=dst, send_sem=send, recv_sem=recv,
            device_id=device, device_id_type=MESH,
        )

    def along_y(i):
        return (v, ((y + i) % YD) * ZD + z)

    def along_z(i):
        return (v, y * ZD + (z + i) % ZD)

    barrier = pltpu.get_barrier_semaphore()
    for i in range(1, 8):
        for device in (along_y(i), along_z(i)):
            pl.semaphore_signal(barrier, inc=1, device_id=device, device_id_type=MESH)
    for other in (v_next, v_prev, v_twin):
        pl.semaphore_signal(barrier, inc=1, device_id=(other, f), device_id_type=MESH)

    own_q[...] = wq_mine[...]
    own_k[...] = wk_mine[:, lanes(v)]
    wq[v, y, z] = own_q[...]
    wk[v, y, z] = own_k[...]
    wo[v] = wo_mine[...]
    low = lax.broadcasted_iota(jnp.int32, (8, 8, D), 1) < 4

    def lay_out(i, carry):
        first = tok[0, rows_at(64 * i, 64), :].astype(F32).reshape(8, 8, D)
        second = tok[1, rows_at(64 * i, 64), :].astype(F32).reshape(8, 8, D)
        even = jnp.where(low, first, pltpu.roll(second, 4, 1))
        odd = jnp.where(low, pltpu.roll(first, 4, 1), second)
        both = jnp.stack([even, odd], axis=1).reshape(16, 8, D)
        halves = jnp.concatenate([both[:, :, :512], both[:, :, 512:]], axis=1)
        tx1[rows_at(16 * i, 16)] = halves.astype(BF16)
        return carry

    lax.fori_loop(0, 4, lay_out, 0)
    rx1[f] = tx1[f]
    pl.semaphore_wait(barrier, 17)
    for i in NEAR:
        pl.semaphore_signal(row_in, inc=1, device_id=along_y(i), device_id_type=MESH)

    def q_piece(core, i, block):
        if core == 0:
            return wq.at[block, (y + i) % YD]
        return wq.at[block, :, (z + i) % ZD]

    def whole(ref, block):
        return ref.at[block]

    def half(ref, number, block):
        if ref is wo:
            return wo.at[block, pl.ds(512 * number, 512)]
        return ref.at[block, pl.ds(4 * number, 4)]

    def plane_first(core, ref, mine, number):
        here = ref.at[v, y, z]
        for i in NEAR:
            remote(mine, here, s_plane.at[number], r_plane.at[number],
                   along_z(i) if core == 0 else along_y(i)).start()

    def seven(core, ref):
        if core == 0:
            return ref.at[v, 0, pl.ds(0, 7)]
        return ref.at[v, pl.ds(0, 7), 0]

    def plane_first_wait(core, ref, number):
        span = seven(core, ref)
        remote(span, span, s_plane.at[number], r_plane.at[number], (v, f)).wait_recv()

    def send_tokens(src, dst, number, to_y, to_z):
        g = to_y * ZD + to_z
        remote(src.at[g], dst.at[f], s_tokens.at[number], r_tokens.at[number], (v, g)).start()

    def send_updated(to_y, to_z):
        g = to_y * ZD + to_z
        remote(tx2.at[g], rx2.at[f], s_tokens.at[1], r_quarter.at[y // 2], (v, g)).start()

    def tokens_wait(dst, number):
        span = dst.at[pl.ds(0, FRAMES - 1)]
        remote(span, span, s_tokens.at[number], r_tokens.at[number], (v, f)).wait_recv()

    groups = {"q": (0, wq), "o": (1, wo), "k": (2, wk)}
    moves = [
        (0, v, v_prev, v_next), (1, v, v_prev, v_next),
        (0, v, v_next, v_prev), (1, v, v_next, v_prev),
        (0, v_prev, v_far, v_next), (1, v_next, v_far, v_prev),
        (None, v, v_twin, v_twin),
        (None, v_prev, 2 * x_prev + 1 - c, v_twin),
        (None, v_next, 2 * x_next + 1 - c, v_twin),
        (0, v_far, 2 * x_far + 1 - c, v_twin), (1, v_far, 2 * x_far + 1 - c, v_twin),
    ]

    def view(name, part, block):
        ref = groups[name][1]
        return whole(ref, block) if part is None else half(ref, part, block)

    def move(name, number):
        group = groups[name][0]
        part, block, _, target = moves[number]
        here = view(name, part, block)
        return remote(here, here, s_span.at[group, number], r_span.at[group, number], (target, f))

    def start(name, *numbers):
        for number in numbers:
            move(name, number).start()

    def arrive(name, *numbers):
        group = groups[name][0]
        for number in numbers:
            part, _, block, target = moves[number]
            here = view(name, part, block)
            remote(
                here, here, s_span.at[group, number], r_span.at[group, number], (target, f)
            ).wait_recv()

    def own_moves(name):
        start(name, 0, 3, 1, 2, 6)

    def forward_moves(name):
        arrive(name, 0)
        start(name, 4)
        arrive(name, 3)
        start(name, 5)
        arrive(name, 1)
        start(name, 7)
        arrive(name, 2)
        start(name, 8)

    def far_moves(name):
        arrive(name, 4)
        start(name, 9)
        arrive(name, 5)
        start(name, 10)

    def twin_moves(name):
        arrive(name, 6, 7, 8, 9, 10)

    def gather(core):
        order = (0,) + NEAR
        plane_first(core, wq, own_q, 0)
        plane_first(core, wk, own_k, 1)
        own_moves("o")
        plane_first_wait(core, wq, 0)

        def send_x(position):
            i = -order[position] % 8
            here = q_piece(core, i, v)
            remote(here, here, s_span.at[0, 0], r_piece.at[1, position], (v_next, f)).start()
            remote(here, here, s_span.at[0, 1], r_piece.at[2, position], (v_prev, f)).start()

        def arrived(column, position, block):
            here = q_piece(core, -order[position] % 8, block)
            remote(here, here, s_span.at[0, 0], r_piece.at[column, position], (v, f)).wait_recv()

        def forward(position):
            arrived(1, position, v_prev)
            if position % 2 == 0:
                here = q_piece(core, -order[position] % 8, v_prev)
                remote(here, here, s_span.at[0, 2], r_piece.at[3, position], (v_next, f)).start()
            arrived(2, position, v_next)
            if position % 2 == 1:
                here = q_piece(core, -order[position] % 8, v_next)
                remote(here, here, s_span.at[0, 2], r_piece.at[3, position], (v_prev, f)).start()

        step = along_y if core == 0 else along_z

        def hand_on(position):
            i = order[position]
            here = q_piece(core, -i % 8, v)
            if position == 0:
                onward = ((1, 1, 2), (7, 2, 4))
            elif i < 4:
                onward = ((1, position + 2 if i < 3 else 7, 2),)
            elif i > 5:
                onward = ((7, position + 2, 4),)
            else:
                onward = ()
            for towards, place, number in onward:
                remote(here, here, s_plane.at[number], r_piece.at[0, place], step(towards)).start()

        def some_tokens(part):
            for other in TURNS[8 * part : 8 * part + 8]:
                send_tokens(tx1, rx1, 0, (y + other // ZD) % YD, (z + other % ZD) % ZD)

        hand_on(0)
        send_x(0)
        pl.semaphore_wait(row_in, 7)
        some_tokens(0)
        for position in range(1, 8):
            some_tokens(position)
            arrived(0, position, v)
            hand_on(position)
            send_x(position)
            if position == 5:
                forward_moves("o")
            if position >= 3:
                forward(position - 3)
        start("q", 6)
        plane_first_wait(core, wk, 1)
        for position in range(5, 8):
            forward(position)
        start("q", 7, 8)
        pass

    @pl.when(c == 0)
    def _():
        gather(0)

    @pl.when(c == 1)
    def _():
        gather(1)

    def far_pieces(core):
        for position in range(8):
            here = q_piece(core, -((0,) + NEAR)[position] % 8, v_far)
            remote(here, here, s_span.at[0, 0], r_piece.at[3, position], (v, f)).wait_recv()
            remote(here, here, s_span.at[0, 3], r_piece.at[4, position], (v_twin, f)).start()

    slot_row = owners[...]
    frame_row = frame_ids[...].astype(F32)
    sub = lax.broadcasted_iota(jnp.int32, (SLOTS, SLOTS), 0)
    lane = lax.broadcasted_iota(jnp.int32, (SLOTS, SLOTS), 1)
    place = jnp.where(sub == slot_row, 1.0, 0.0)
    time_col = jnp.sum(place * frame_row, axis=1, keepdims=True)
    time_row = jnp.sum(jnp.where(sub == lane, time_col, 0.0), axis=0, keepdims=True)
    count = counts[0].astype(F32)
    distance = jnp.abs(time_col - time_row)
    valid_col = time_col < count

    for h in range(HEADS):
        bias[h // 2, :, 128 * (h % 2) : 128 * (h % 2) + 128] = jnp.where(
            valid_col, -slopes[h] * distance, -1e30
        )
    row_slot = lax.broadcasted_iota(jnp.int32, (SLOTS, ROWS), 1) // POS
    slot_col = jnp.sum(
        jnp.where(sub == lane, slot_row.astype(F32), 0.0), axis=1, keepdims=True
    )
    owner = jnp.sum(
        jnp.where(row_slot == lax.broadcasted_iota(jnp.int32, (SLOTS, ROWS), 0), slot_col, 0.0),
        axis=0, keepdims=True,
    ).astype(jnp.int32)
    row_pos = lax.broadcasted_iota(jnp.int32, (1, ROWS), 1) % POS
    to_attend = row_pos * SLOTS + owner
    to_send = owner * POS + row_pos
    out_row = lax.broadcasted_iota(jnp.int32, (128, ROWS), 0)

    tokens_wait(rx1, 0)

    def k_plane(core):
        mine_k = wk.at[v, y] if core == 0 else wk.at[v, :, z]
        for i in NEAR:
            remote(mine_k, mine_k, s_plane.at[3], r_plane.at[3],
                   along_y(i) if core == 0 else along_z(i)).start()

    @pl.when(c == 0)
    def _():
        k_plane(0)

    @pl.when(c == 1)
    def _():
        k_plane(1)

    def unpack(i, carry):
        blocks = rx1[rows_at(8 * i, 8)].astype(F32)
        held[rows_at(64 * i, 64), :512] = blocks[:, :8].reshape(64, 512).astype(BF16)
        held[rows_at(64 * i, 64), 512:] = blocks[:, 8:].reshape(64, 512).astype(BF16)
        return carry

    lax.fori_loop(0, 8, unpack, 0)

    def place_and_norm(p, carry):
        here = rows_at(128 * p, 128)
        picked = jnp.dot(
            one_hot(out_row + p * 128, to_attend), held[...], preferred_element_type=F32
        )
        normed[here] = norm(picked, gain1[...])
        resid[here] = jnp.dot(
            one_hot(out_row + p * 128, to_send), held[...], preferred_element_type=F32
        ).astype(BF16)
        return carry

    lax.fori_loop(0, POS, place_and_norm, 0)

    arrive("q", 6, 7, 8)
    flat = wq.reshape(8, 3 * D, 128)
    near = (2 * x, 2 * x + 1, 2 * x_prev, 2 * x_prev + 1, 2 * x_next, 2 * x_next + 1)
    far = (2 * x_far, 2 * x_far + 1)

    def features(blocks):
        return jnp.concatenate([normed[:, lanes(block)] for block in blocks], axis=1)

    def weights_rows(start, j, blocks):
        here = pl.ds(pl.multiple_of(start + 512 * j, 512), 512)
        return jnp.concatenate([flat[block, here] for block in blocks], axis=1)

    def project_near(j, carry):
        here = rows_at(512 * j, 512)
        rows = features(near)
        part_q[here] = lax.dot_general(
            weights_rows(0, j, near), rows, NT, preferred_element_type=F32
        )
        part_v[here] = lax.dot_general(
            weights_rows(2048, j, near), rows, NT, preferred_element_type=F32
        )
        part_k[:, here] = lax.dot_general(
            rows, weights_rows(1024, j, near), NT, preferred_element_type=F32
        )
        return carry

    lax.fori_loop(0, 2, project_near, 0)

    @pl.when(c == 0)
    def _():
        far_pieces(0)

    @pl.when(c == 1)
    def _():
        far_pieces(1)

    for position in range(8):
        here = wq.at[v_twin, 0]
        remote(here, here, s_span.at[0, 3], r_piece.at[4, position], (v_twin, f)).wait_recv()

    def project(j, carry):
        here = rows_at(512 * j, 512)
        rows = features(far)
        query = part_q[here] + lax.dot_general(
            weights_rows(0, j, far), rows, NT, preferred_element_type=F32
        )
        query_t[here] = (query.astype(BF16) * 0.125).astype(BF16)
        value = part_v[here] + lax.dot_general(
            weights_rows(2048, j, far), rows, NT, preferred_element_type=F32
        )
        value_t[here] = value.astype(BF16)
        key = part_k[:, here] + lax.dot_general(
            rows, weights_rows(1024, j, far), NT, preferred_element_type=F32
        )
        keyed[:, here] = key.astype(BF16)
        return carry

    lax.fori_loop(0, 2, project, 0)
    far_moves("o")
    span = wk.at[v, pl.ds(0, 7)]
    remote(span, span, s_plane.at[3], r_plane.at[3], (v, f)).wait_recv()
    own_moves("k")

    blank = jnp.zeros((64, 128), BF16)
    ones = jnp.ones((16, 128), BF16)

    def attend(p, carry):
        here = rows_at(SLOTS * p, SLOTS)
        for pair in range(8):
            top, bottom = pl.ds(128 * pair, 64), pl.ds(128 * pair + 64, 64)
            queries = jnp.concatenate([
                jnp.concatenate([query_t[top, here], blank], axis=1),
                jnp.concatenate([blank, query_t[bottom, here]], axis=1),
            ], axis=0)
            scores = jnp.dot(
                keyed[here, 128 * pair : 128 * pair + 128], queries, preferred_element_type=F32
            ) + bias[pair]
            expo = jnp.exp(scores - jnp.max(scores, axis=0, keepdims=True)).astype(BF16)
            values = jnp.concatenate([value_t[pl.ds(128 * pair, 128), here], ones], axis=0)
            summed = jnp.dot(values, expo, preferred_element_type=F32)
            scale = 1.0 / summed[128:129]
            attended_t[top, here] = (summed[:64, :128] * scale[:, :128]).astype(BF16)
            attended_t[bottom, here] = (summed[64:128, 128:] * scale[:, 128:]).astype(BF16)
        return carry

    lax.fori_loop(0, POS, attend, 0)
    twin_moves("o")

    column = lax.broadcasted_iota(jnp.int32, (1, ROWS), 1)
    from_attend = (column % SLOTS) * POS + column // SLOTS

    for i in range(4):
        quarter = (y // 2 + i) % 4
        here = rows_at(128 * quarter, 128)
        moved = lax.dot_general(
            one_hot(out_row + 128 * quarter, from_attend), attended_t[...], NT,
            preferred_element_type=F32,
        ).astype(BF16)
        out_weight = jnp.concatenate([wo[block] for block in range(8)], axis=1)
        added = jnp.dot(moved, out_weight, preferred_element_type=F32)
        both = (resid[here].astype(F32) + added).reshape(16, 8, D)
        halves = jnp.concatenate([both[:, :, :512], both[:, :, 512:]], axis=1)
        tx2[rows_at(16 * quarter, 16)] = halves.astype(BF16)
        for k in range(8):
            to_z = (z + k) % ZD
            if i == 0:
                if k:
                    send_updated(y, to_z)
                send_updated(y // 2 * 2 + 1 - y % 2, to_z)
            else:
                send_updated(2 * quarter, to_z)
                send_updated(2 * quarter + 1, to_z)

    rx2[f] = tx2[f]
    forward_moves("k")
    far_moves("k")
    twin_moves("k")
    kept = jnp.where(valid_col, 1.0, 0.0)
    slot_sub = lax.broadcasted_iota(jnp.int32, (SLOTS, 1), 0)
    kept_first = jnp.sum(jnp.where(slot_sub == 2 * f, kept, 0.0), axis=0, keepdims=True)
    kept_second = jnp.sum(jnp.where(slot_sub == 2 * f + 1, kept, 0.0), axis=0, keepdims=True)
    row_kept = jnp.where(
        lax.broadcasted_iota(jnp.int32, (128, 1), 0) < 64, kept_first, kept_second
    ) > 0.5

    for i in range(4):
        quarter = (y // 2 + 4 - i) % 4
        span = rx2.at[pl.ds(0, 15 if i == 0 else 16)]
        remote(span, span, s_tokens.at[1], r_quarter.at[quarter], (v, f)).wait_recv()
        blocks = rx2[rows_at(16 * quarter, 16)].astype(F32)
        both = jnp.concatenate([blocks[:, :8], blocks[:, 8:]], axis=2).reshape(8, 2, 8, D)
        even, odd = both[:, 0], both[:, 1]
        first = jnp.where(low, even, pltpu.roll(odd, 4, 1)).reshape(64, D)
        second = jnp.where(low, pltpu.roll(even, 4, 1), odd).reshape(64, D)
        rows = norm(jnp.concatenate([first, second], axis=0), gain2[...])
        for j in range(4):
            weight = jnp.concatenate(
                [wk[block, pl.ds(2 * j, 2)].reshape(512, 128) for block in range(8)], axis=1
            )
            result = lax.dot_general(rows, weight, NT, preferred_element_type=F32)
            result = jnp.where(row_kept, result, 0.0).astype(BF16)
            out = keys_out if j < 2 else values_out
            out[rows_at(64 * quarter, 64), pl.ds(512 * (j % 2), 512)] = result[:64]
            out[pl.ds(pl.multiple_of(256 + 64 * quarter, 64), 64), pl.ds(512 * (j % 2), 512)] = result[64:]

    def sent(span, semaphore):
        remote(span, span, semaphore, r_plane.at[0], (v, f)).wait_send()

    for name, numbers in (("q", (6, 7, 8)), ("o", range(11)), ("k", range(11))):
        for number in numbers:
            move(name, number).wait_send()
    for number in range(4):
        sent(whole(wq, v), s_span.at[0, number])
    sent(wq.at[v, 0, pl.ds(0, 7)], s_plane.at[0])
    sent(wk.at[v, 0, pl.ds(0, 7)], s_plane.at[1])
    sent(wq.at[v, pl.ds(0, 4)], s_plane.at[2])
    sent(wq.at[v, pl.ds(0, 3)], s_plane.at[4])
    sent(wk.at[v, pl.ds(0, 7)], s_plane.at[3])
    for number in range(2):
        sent(rx1.at[pl.ds(0, FRAMES - 1)], s_tokens.at[number])


def body(tokens, counts, frame_index, owner_slot, gain_attn, gain_kv, slopes, w_qkv, w_out, w_kv):
    vmem = pl.BlockSpec(memory_space=pltpu.VMEM)
    smem = pl.BlockSpec(memory_space=pltpu.SMEM)
    dma = pltpu.SemaphoreType.DMA
    keys, values = pl.pallas_call(
        kernel,
        out_shape=(
            jax.ShapeDtypeStruct((ROWS, D), BF16),
            jax.ShapeDtypeStruct((ROWS, D), BF16),
        ),
        in_specs=[vmem] * 4 + [smem] + [vmem] * 4 + [smem],
        out_specs=(vmem, vmem),
        scratch_shapes=[
            pltpu.VMEM((8, YD, ZD, 48, 128), BF16),
            pltpu.VMEM((8, YD, ZD, 32, 128), BF16),
            pltpu.VMEM((8, D, 128), BF16),
            *[pltpu.VMEM((FRAMES, 16, 512), BF16) for _ in range(4)],
            pltpu.VMEM((ROWS, D), BF16),
            pltpu.VMEM((ROWS, D), BF16),
            pltpu.VMEM((ROWS, D), BF16),
            pltpu.VMEM((D, ROWS), BF16),
            pltpu.VMEM((ROWS, D), BF16),
            pltpu.VMEM((D, ROWS), BF16),
            pltpu.VMEM((D, ROWS), BF16),
            pltpu.VMEM((8, SLOTS, 256), F32),
            pltpu.VMEM((48, 128), BF16),
            pltpu.VMEM((32, 128), BF16),
            pltpu.VMEM((D, ROWS), F32),
            pltpu.VMEM((ROWS, D), F32),
            pltpu.VMEM((D, ROWS), F32),
            dma((5,)), dma((4,)), dma((5, 8)), dma((3, 11)), dma((3, 11)), dma((2,)), dma((1,)), dma((4,)),
            pltpu.SemaphoreType.REGULAR,
        ],
        compiler_params=pltpu.CompilerParams(
            collective_id=0, has_side_effects=True, vmem_limit_bytes=VMEM_MIB * 2**20
        ),
    )(
        tokens[0], w_qkv.T, w_kv.T, w_out, counts, frame_index, owner_slot,
        gain_attn.reshape(1, D), gain_kv.reshape(1, D), slopes,
    )
    return keys.reshape(1, 2, 256, D), values.reshape(1, 2, 256, D)


def solution(mesh):
    return jax.shard_map(
        body,
        mesh=mesh,
        in_specs=(
            P("video", "frame", None, None),
            P("video"),
            P("video", None),
            P("video", None),
            P(),
            P(),
            P(),
            P("video", "frame"),
            P(None, "video"),
            P(None, "frame"),
        ),
        out_specs=(P("video", "frame", None, None), P("video", "frame", None, None)),
        check_vma=False,
    )
```

```python
import functools
import jax
import jax.numpy as jnp
from jax import lax
from jax.experimental import pallas as pl
from jax.experimental.pallas import tpu as pltpu
from jax.sharding import PartitionSpec as P

XD, YD, ZD = 4, 8, 8
FRAMES = YD * ZD
SLOTS = 2 * FRAMES
POS = 4
ROWS = POS * SLOTS
D = 1024
HEADS = 16
NEAR = (1, 7, 2, 6, 3, 5, 4)
STEPS = sorted(
    range(1, FRAMES), key=lambda k: min(k // ZD, YD - k // ZD) + min(k % ZD, ZD - k % ZD)
)
TURNS = [k for pair in zip(STEPS[::-1], STEPS) for k in pair][: FRAMES - 1]
VMEM_MIB = 60
MESH = pl.DeviceIdType.MESH
NT = (((1,), (1,)), ((), ()))
F32 = jnp.float32
BF16 = jnp.bfloat16


def lanes(block):
    return pl.ds(pl.multiple_of(block * 128, 128), 128)


def rows_at(start, count):
    return pl.ds(pl.multiple_of(start, count), count)


def norm(values, gain):
    center = jnp.mean(values, axis=-1, keepdims=True)
    shifted = values - center
    spread = jnp.mean(jnp.square(shifted), axis=-1, keepdims=True)
    return (shifted * lax.rsqrt(spread + 1e-05) * gain).astype(BF16)


def one_hot(rows, row_of_column):
    return jnp.where(rows == row_of_column, 1.0, 0.0).astype(BF16)


def kernel(
    tok_in, wq_mine, wk_mine, wo_mine, counts, frame_ids, owners, gain1, gain2, slopes,
    keys_out, values_out,
    wq, wk, wo, tx1, rx1, tx2, rx2, held, resid, normed, query_t, keyed, value_t,
    attended_t, bias, tok, own, part_q, part_k, part_v,
    s_plane, r_plane, r_piece, s_span, r_span, s_tokens, r_tokens, r_quarter, row_in,
):
    v = lax.axis_index("video")
    f = lax.axis_index("frame")
    x, c = v // 2, v % 2
    y, z = f // ZD, f % ZD
    x_next, x_prev, x_far = (x + 1) % XD, (x + 3) % XD, (x + 2) % XD
    v_next, v_prev, v_far = 2 * x_next + c, 2 * x_prev + c, 2 * x_far + c
    v_twin = 2 * x + 1 - c

    def remote(src, dst, send, recv, device):
        return pltpu.make_async_remote_copy(
            src_ref=src, dst_ref=dst, send_sem=send, recv_sem=recv,
            device_id=device, device_id_type=MESH,
        )

    def along_y(i):
        return (v, ((y + i) % YD) * ZD + z)

    def along_z(i):
        return (v, y * ZD + (z + i) % ZD)

    loads = [
        pltpu.make_async_copy(src, dst, own.at[number])
        for number, (src, dst) in enumerate((
            (wq_mine, wq.at[v, y, z]), (wk_mine.at[:, lanes(v)], wk.at[v, y, z]),
            (wo_mine, wo.at[v]), (tok_in, tok),
        ))
    ]
    for load in loads:
        load.start()

    barrier = pltpu.get_barrier_semaphore()
    for i in range(1, 8):
        for device in (along_y(i), along_z(i)):
            pl.semaphore_signal(barrier, inc=1, device_id=device, device_id_type=MESH)
    for other in (v_next, v_prev, v_twin):
        pl.semaphore_signal(barrier, inc=1, device_id=(other, f), device_id_type=MESH)

    for load in loads:
        load.wait()
    low = lax.broadcasted_iota(jnp.int32, (8, 8, D), 1) < 4

    def lay_out(i, carry):
        first = tok[0, rows_at(64 * i, 64), :].astype(F32).reshape(8, 8, D)
        second = tok[1, rows_at(64 * i, 64), :].astype(F32).reshape(8, 8, D)
        even = jnp.where(low, first, pltpu.roll(second, 4, 1))
        odd = jnp.where(low, pltpu.roll(first, 4, 1), second)
        both = jnp.stack([even, odd], axis=1).reshape(16, 8, D)
        halves = jnp.concatenate([both[:, :, :512], both[:, :, 512:]], axis=1)
        tx1[rows_at(16 * i, 16)] = halves.astype(BF16)
        return carry

    lax.fori_loop(0, 4, lay_out, 0)
    rx1[f] = tx1[f]
    pl.semaphore_wait(barrier, 17)
    for i in NEAR:
        pl.semaphore_signal(row_in, inc=1, device_id=along_y(i), device_id_type=MESH)

    def q_piece(core, i, block):
        if core == 0:
            return wq.at[block, (y + i) % YD]
        return wq.at[block, :, (z + i) % ZD]

    def whole(ref, block):
        return ref.at[block]

    def half(ref, number, block):
        if ref is wo:
            return wo.at[block, pl.ds(512 * number, 512)]
        return ref.at[block, pl.ds(4 * number, 4)]

    def plane_first(core, ref, number):
        here = ref.at[v, y, z]
        for i in NEAR:
            remote(here, here, s_plane.at[number], r_plane.at[number],
                   along_z(i) if core == 0 else along_y(i)).start()

    def seven(core, ref):
        if core == 0:
            return ref.at[v, 0, pl.ds(0, 7)]
        return ref.at[v, pl.ds(0, 7), 0]

    def plane_first_wait(core, ref, number):
        span = seven(core, ref)
        remote(span, span, s_plane.at[number], r_plane.at[number], (v, f)).wait_recv()

    def send_tokens(src, dst, number, to_y, to_z):
        g = to_y * ZD + to_z
        remote(src.at[g], dst.at[f], s_tokens.at[number], r_tokens.at[number], (v, g)).start()

    def send_updated(to_y, to_z):
        g = to_y * ZD + to_z
        remote(tx2.at[g], rx2.at[f], s_tokens.at[1], r_quarter.at[y // 2], (v, g)).start()

    def tokens_wait(dst, number):
        span = dst.at[pl.ds(0, FRAMES - 1)]
        remote(span, span, s_tokens.at[number], r_tokens.at[number], (v, f)).wait_recv()

    groups = {"q": (0, wq), "o": (1, wo), "k": (2, wk)}
    moves = [
        (0, v, v_prev, v_next), (1, v, v_prev, v_next),
        (0, v, v_next, v_prev), (1, v, v_next, v_prev),
        (0, v_prev, v_far, v_next), (1, v_next, v_far, v_prev),
        (None, v, v_twin, v_twin),
        (None, v_prev, 2 * x_prev + 1 - c, v_twin),
        (None, v_next, 2 * x_next + 1 - c, v_twin),
        (0, v_far, 2 * x_far + 1 - c, v_twin), (1, v_far, 2 * x_far + 1 - c, v_twin),
    ]

    def view(name, part, block):
        ref = groups[name][1]
        return whole(ref, block) if part is None else half(ref, part, block)

    def move(name, number):
        group = groups[name][0]
        part, block, _, target = moves[number]
        here = view(name, part, block)
        return remote(here, here, s_span.at[group, number], r_span.at[group, number], (target, f))

    def start(name, *numbers):
        for number in numbers:
            move(name, number).start()

    def arrive(name, *numbers):
        group = groups[name][0]
        for number in numbers:
            part, _, block, target = moves[number]
            here = view(name, part, block)
            remote(
                here, here, s_span.at[group, number], r_span.at[group, number], (target, f)
            ).wait_recv()

    def own_moves(name):
        start(name, 0, 3, 1, 2, 6)

    def forward_moves(name):
        arrive(name, 0)
        start(name, 4)
        arrive(name, 3)
        start(name, 5)
        arrive(name, 1)
        start(name, 7)
        arrive(name, 2)
        start(name, 8)

    def far_moves(name):
        arrive(name, 4)
        start(name, 9)
        arrive(name, 5)
        start(name, 10)

    def twin_moves(name):
        arrive(name, 6, 7, 8, 9, 10)

    def gather(core):
        order = (0,) + NEAR
        plane_first(core, wq, 0)
        plane_first(core, wk, 1)
        own_moves("o")
        plane_first_wait(core, wq, 0)

        def send_x(position):
            i = -order[position] % 8
            here = q_piece(core, i, v)
            remote(here, here, s_span.at[0, 0], r_piece.at[1, position], (v_next, f)).start()
            remote(here, here, s_span.at[0, 1], r_piece.at[2, position], (v_prev, f)).start()

        def arrived(column, position, block):
            here = q_piece(core, -order[position] % 8, block)
            remote(here, here, s_span.at[0, 0], r_piece.at[column, position], (v, f)).wait_recv()

        def forward(position):
            arrived(1, position, v_prev)
            if position % 2 == 0:
                here = q_piece(core, -order[position] % 8, v_prev)
                remote(here, here, s_span.at[0, 2], r_piece.at[3, position], (v_next, f)).start()
            arrived(2, position, v_next)
            if position % 2 == 1:
                here = q_piece(core, -order[position] % 8, v_next)
                remote(here, here, s_span.at[0, 2], r_piece.at[3, position], (v_prev, f)).start()

        step = along_y if core == 0 else along_z

        def hand_on(position):
            i = order[position]
            here = q_piece(core, -i % 8, v)
            if position == 0:
                onward = ((1, 1, 2), (7, 2, 4))
            elif i < 4:
                onward = ((1, position + 2 if i < 3 else 7, 2),)
            elif i > 5:
                onward = ((7, position + 2, 4),)
            else:
                onward = ()
            for towards, place, number in onward:
                remote(here, here, s_plane.at[number], r_piece.at[0, place], step(towards)).start()

        def some_tokens(part):
            for other in TURNS[8 * part : 8 * part + 8]:
                send_tokens(tx1, rx1, 0, (y + other // ZD) % YD, (z + other % ZD) % ZD)

        hand_on(0)
        send_x(0)
        pl.semaphore_wait(row_in, 7)
        some_tokens(0)
        for position in range(1, 8):
            some_tokens(position)
            arrived(0, position, v)
            hand_on(position)
            send_x(position)
            if position == 5:
                forward_moves("o")
            if position >= 3:
                forward(position - 3)
        start("q", 6)
        plane_first_wait(core, wk, 1)
        for position in range(5, 8):
            forward(position)
        start("q", 7, 8)
        pass

    @pl.when(c == 0)
    def _():
        gather(0)

    @pl.when(c == 1)
    def _():
        gather(1)

    def far_pieces(core):
        for position in range(8):
            here = q_piece(core, -((0,) + NEAR)[position] % 8, v_far)
            remote(here, here, s_span.at[0, 0], r_piece.at[3, position], (v, f)).wait_recv()
            remote(here, here, s_span.at[0, 3], r_piece.at[4, position], (v_twin, f)).start()

    slot_row = owners[...]
    frame_row = frame_ids[...].astype(F32)
    sub = lax.broadcasted_iota(jnp.int32, (SLOTS, SLOTS), 0)
    lane = lax.broadcasted_iota(jnp.int32, (SLOTS, SLOTS), 1)
    place = jnp.where(sub == slot_row, 1.0, 0.0)
    time_col = jnp.sum(place * frame_row, axis=1, keepdims=True)
    time_row = jnp.sum(jnp.where(sub == lane, time_col, 0.0), axis=0, keepdims=True)
    count = counts[0].astype(F32)
    distance = jnp.abs(time_col - time_row)
    valid_col = time_col < count

    for h in range(HEADS):
        bias[h // 2, :, 128 * (h % 2) : 128 * (h % 2) + 128] = jnp.where(
            valid_col, -slopes[h] * distance, -1e30
        )
    row_slot = lax.broadcasted_iota(jnp.int32, (SLOTS, ROWS), 1) // POS
    slot_col = jnp.sum(
        jnp.where(sub == lane, slot_row.astype(F32), 0.0), axis=1, keepdims=True
    )
    owner = jnp.sum(
        jnp.where(row_slot == lax.broadcasted_iota(jnp.int32, (SLOTS, ROWS), 0), slot_col, 0.0),
        axis=0, keepdims=True,
    ).astype(jnp.int32)
    row_pos = lax.broadcasted_iota(jnp.int32, (1, ROWS), 1) % POS
    to_attend = row_pos * SLOTS + owner
    to_send = owner * POS + row_pos
    out_row = lax.broadcasted_iota(jnp.int32, (128, ROWS), 0)

    tokens_wait(rx1, 0)

    def k_plane(core):
        mine_k = wk.at[v, y] if core == 0 else wk.at[v, :, z]
        for i in NEAR:
            remote(mine_k, mine_k, s_plane.at[3], r_plane.at[3],
                   along_y(i) if core == 0 else along_z(i)).start()

    @pl.when(c == 0)
    def _():
        k_plane(0)

    @pl.when(c == 1)
    def _():
        k_plane(1)

    def unpack(i, carry):
        blocks = rx1[rows_at(8 * i, 8)].astype(F32)
        held[rows_at(64 * i, 64), :512] = blocks[:, :8].reshape(64, 512).astype(BF16)
        held[rows_at(64 * i, 64), 512:] = blocks[:, 8:].reshape(64, 512).astype(BF16)
        return carry

    lax.fori_loop(0, 8, unpack, 0)

    def place_and_norm(p, carry):
        here = rows_at(128 * p, 128)
        picked = jnp.dot(
            one_hot(out_row + p * 128, to_attend), held[...], preferred_element_type=F32
        )
        normed[here] = norm(picked, gain1[...])
        resid[here] = jnp.dot(
            one_hot(out_row + p * 128, to_send), held[...], preferred_element_type=F32
        ).astype(BF16)
        return carry

    lax.fori_loop(0, POS, place_and_norm, 0)

    arrive("q", 6, 7, 8)
    flat = wq.reshape(8, 3 * D, 128)
    near = (2 * x, 2 * x + 1, 2 * x_prev, 2 * x_prev + 1, 2 * x_next, 2 * x_next + 1)
    far = (2 * x_far, 2 * x_far + 1)

    def features(blocks):
        return jnp.concatenate([normed[:, lanes(block)] for block in blocks], axis=1)

    def weights_rows(start, j, blocks):
        here = pl.ds(pl.multiple_of(start + 512 * j, 512), 512)
        return jnp.concatenate([flat[block, here] for block in blocks], axis=1)

    def project_near(j, carry):
        here = rows_at(512 * j, 512)
        rows = features(near)
        part_q[here] = lax.dot_general(
            weights_rows(0, j, near), rows, NT, preferred_element_type=F32
        )
        part_v[here] = lax.dot_general(
            weights_rows(2048, j, near), rows, NT, preferred_element_type=F32
        )
        part_k[:, here] = lax.dot_general(
            rows, weights_rows(1024, j, near), NT, preferred_element_type=F32
        )
        return carry

    lax.fori_loop(0, 2, project_near, 0)

    @pl.when(c == 0)
    def _():
        far_pieces(0)

    @pl.when(c == 1)
    def _():
        far_pieces(1)

    for position in range(8):
        here = wq.at[v_twin, 0]
        remote(here, here, s_span.at[0, 3], r_piece.at[4, position], (v_twin, f)).wait_recv()

    def project(j, carry):
        here = rows_at(512 * j, 512)
        rows = features(far)
        query = part_q[here] + lax.dot_general(
            weights_rows(0, j, far), rows, NT, preferred_element_type=F32
        )
        query_t[here] = (query.astype(BF16) * 0.125).astype(BF16)
        value = part_v[here] + lax.dot_general(
            weights_rows(2048, j, far), rows, NT, preferred_element_type=F32
        )
        value_t[here] = value.astype(BF16)
        key = part_k[:, here] + lax.dot_general(
            rows, weights_rows(1024, j, far), NT, preferred_element_type=F32
        )
        keyed[:, here] = key.astype(BF16)
        return carry

    lax.fori_loop(0, 2, project, 0)
    far_moves("o")
    span = wk.at[v, pl.ds(0, 7)]
    remote(span, span, s_plane.at[3], r_plane.at[3], (v, f)).wait_recv()
    own_moves("k")

    blank = jnp.zeros((64, 128), BF16)
    ones = jnp.ones((16, 128), BF16)

    def attend(p, carry):
        here = rows_at(SLOTS * p, SLOTS)
        for pair in range(8):
            top, bottom = pl.ds(128 * pair, 64), pl.ds(128 * pair + 64, 64)
            queries = jnp.concatenate([
                jnp.concatenate([query_t[top, here], blank], axis=1),
                jnp.concatenate([blank, query_t[bottom, here]], axis=1),
            ], axis=0)
            scores = jnp.dot(
                keyed[here, 128 * pair : 128 * pair + 128], queries, preferred_element_type=F32
            ) + bias[pair]
            expo = jnp.exp(scores - jnp.max(scores, axis=0, keepdims=True)).astype(BF16)
            values = jnp.concatenate([value_t[pl.ds(128 * pair, 128), here], ones], axis=0)
            summed = jnp.dot(values, expo, preferred_element_type=F32)
            scale = 1.0 / summed[128:129]
            attended_t[top, here] = (summed[:64, :128] * scale[:, :128]).astype(BF16)
            attended_t[bottom, here] = (summed[64:128, 128:] * scale[:, 128:]).astype(BF16)
        return carry

    lax.fori_loop(0, POS, attend, 0)
    twin_moves("o")

    column = lax.broadcasted_iota(jnp.int32, (1, ROWS), 1)
    from_attend = (column % SLOTS) * POS + column // SLOTS

    for i in range(4):
        quarter = (y // 2 + i) % 4
        here = rows_at(128 * quarter, 128)
        moved = lax.dot_general(
            one_hot(out_row + 128 * quarter, from_attend), attended_t[...], NT,
            preferred_element_type=F32,
        ).astype(BF16)
        out_weight = jnp.concatenate([wo[block] for block in range(8)], axis=1)
        added = jnp.dot(moved, out_weight, preferred_element_type=F32)
        both = (resid[here].astype(F32) + added).reshape(16, 8, D)
        halves = jnp.concatenate([both[:, :, :512], both[:, :, 512:]], axis=1)
        tx2[rows_at(16 * quarter, 16)] = halves.astype(BF16)
        for k in range(8):
            to_z = (z + k) % ZD
            if i == 0:
                if k:
                    send_updated(y, to_z)
                send_updated(y // 2 * 2 + 1 - y % 2, to_z)
            else:
                send_updated(2 * quarter, to_z)
                send_updated(2 * quarter + 1, to_z)

    rx2[f] = tx2[f]
    forward_moves("k")
    far_moves("k")
    twin_moves("k")
    kept = jnp.where(valid_col, 1.0, 0.0)
    slot_sub = lax.broadcasted_iota(jnp.int32, (SLOTS, 1), 0)
    kept_first = jnp.sum(jnp.where(slot_sub == 2 * f, kept, 0.0), axis=0, keepdims=True)
    kept_second = jnp.sum(jnp.where(slot_sub == 2 * f + 1, kept, 0.0), axis=0, keepdims=True)
    row_kept = jnp.where(
        lax.broadcasted_iota(jnp.int32, (128, 1), 0) < 64, kept_first, kept_second
    ) > 0.5

    for i in range(4):
        quarter = (y // 2 + 4 - i) % 4
        span = rx2.at[pl.ds(0, 15 if i == 0 else 16)]
        remote(span, span, s_tokens.at[1], r_quarter.at[quarter], (v, f)).wait_recv()
        blocks = rx2[rows_at(16 * quarter, 16)].astype(F32)
        both = jnp.concatenate([blocks[:, :8], blocks[:, 8:]], axis=2).reshape(8, 2, 8, D)
        even, odd = both[:, 0], both[:, 1]
        first = jnp.where(low, even, pltpu.roll(odd, 4, 1)).reshape(64, D)
        second = jnp.where(low, pltpu.roll(even, 4, 1), odd).reshape(64, D)
        rows = norm(jnp.concatenate([first, second], axis=0), gain2[...])
        for j in range(4):
            weight = jnp.concatenate(
                [wk[block, pl.ds(2 * j, 2)].reshape(512, 128) for block in range(8)], axis=1
            )
            result = lax.dot_general(rows, weight, NT, preferred_element_type=F32)
            result = jnp.where(row_kept, result, 0.0).astype(BF16)
            out = keys_out if j < 2 else values_out
            out[rows_at(64 * quarter, 64), pl.ds(512 * (j % 2), 512)] = result[:64]
            out[pl.ds(pl.multiple_of(256 + 64 * quarter, 64), 64), pl.ds(512 * (j % 2), 512)] = result[64:]

    def sent(span, semaphore):
        remote(span, span, semaphore, r_plane.at[0], (v, f)).wait_send()

    for name, numbers in (("q", (6, 7, 8)), ("o", range(11)), ("k", range(11))):
        for number in numbers:
            move(name, number).wait_send()
    for number in range(4):
        sent(whole(wq, v), s_span.at[0, number])
    sent(wq.at[v, 0, pl.ds(0, 7)], s_plane.at[0])
    sent(wk.at[v, 0, pl.ds(0, 7)], s_plane.at[1])
    sent(wq.at[v, pl.ds(0, 4)], s_plane.at[2])
    sent(wq.at[v, pl.ds(0, 3)], s_plane.at[4])
    sent(wk.at[v, pl.ds(0, 7)], s_plane.at[3])
    for number in range(2):
        sent(rx1.at[pl.ds(0, FRAMES - 1)], s_tokens.at[number])


def body(tokens, counts, frame_index, owner_slot, gain_attn, gain_kv, slopes, w_qkv, w_out, w_kv):
    vmem = pl.BlockSpec(memory_space=pltpu.VMEM)
    hbm = pl.BlockSpec(memory_space=pltpu.HBM)
    smem = pl.BlockSpec(memory_space=pltpu.SMEM)
    dma = pltpu.SemaphoreType.DMA
    keys, values = pl.pallas_call(
        kernel,
        out_shape=(pltpu.VMEM((ROWS, D), BF16), pltpu.VMEM((ROWS, D), BF16)),
        in_specs=[hbm] * 4 + [smem] + [vmem] * 4 + [smem],
        out_specs=(vmem, vmem),
        scratch_shapes=[
            pltpu.VMEM((8, YD, ZD, 48, 128), BF16),
            pltpu.VMEM((8, YD, ZD, 32, 128), BF16),
            pltpu.VMEM((8, D, 128), BF16),
            *[pltpu.VMEM((FRAMES, 16, 512), BF16) for _ in range(4)],
            pltpu.VMEM((ROWS, D), BF16),
            pltpu.VMEM((ROWS, D), BF16),
            pltpu.VMEM((ROWS, D), BF16),
            pltpu.VMEM((D, ROWS), BF16),
            pltpu.VMEM((ROWS, D), BF16),
            pltpu.VMEM((D, ROWS), BF16),
            pltpu.VMEM((D, ROWS), BF16),
            pltpu.VMEM((8, SLOTS, 256), F32),
            pltpu.VMEM((2, 256, D), BF16),
            dma((4,)),
            pltpu.VMEM((D, ROWS), F32),
            pltpu.VMEM((ROWS, D), F32),
            pltpu.VMEM((D, ROWS), F32),
            dma((5,)), dma((4,)), dma((5, 8)), dma((3, 11)), dma((3, 11)), dma((2,)), dma((1,)), dma((4,)),
            pltpu.SemaphoreType.REGULAR,
        ],
        compiler_params=pltpu.CompilerParams(
            collective_id=0, has_side_effects=True, vmem_limit_bytes=VMEM_MIB * 2**20
        ),
    )(
        tokens[0], w_qkv.T, w_kv.T, w_out, counts, frame_index, owner_slot,
        gain_attn.reshape(1, D), gain_kv.reshape(1, D), slopes,
    )
    return keys.reshape(1, 2, 256, D), values.reshape(1, 2, 256, D)


def solution(mesh):
    return jax.shard_map(
        body,
        mesh=mesh,
        in_specs=(
            P("video", "frame", None, None),
            P("video"),
            P("video", None),
            P("video", None),
            P(),
            P(),
            P(),
            P("video", "frame"),
            P(None, "video"),
            P(None, "frame"),
        ),
        out_specs=(P("video", "frame", None, None), P("video", "frame", None, None)),
        check_vma=False,
    )
```
